32 devices in a mesh: dp: 8 (over z, x), tensor: 4 (over y, core).
Axes of the slice: x: 2, y: 2, z: 4, core: 2. Of those that a mesh axis runs over, the one named last changes fastest.
Arguments:
- tokens: bfloat16 [16, 1024, 768], P('dp'), may hold values from -6 to 6
- cotangent: bfloat16 [16, 1024, 768], P('dp'), may hold values from -6 to 6
- lengths: int32 [16], replicated, may hold values from 64 to 1024, as said below
- perm: int32 [16], replicated, may hold values from 0 to 15, as said below
- norm_gain: float32 [768], replicated, may hold values from 0.5 to 1.5
- proj_gate: bfloat16 [768, 1536], P(None, 'tensor'), may hold values from -0.21875 to 0.21875
- proj_inner: bfloat16 [768, 1536], P(None, 'tensor'), may hold values from -0.21875 to 0.21875
- state_input_matrix: bfloat16 [768, 256], replicated, may hold values from -0.21875 to 0.21875
- stepsize_matrix: bfloat16 [768, 24], P(None, 'tensor'), may hold values from -0.21875 to 0.21875
- conv_weight: float32 [4, 1536], P(None, 'tensor'), may hold values from -3 to 3
- conv_offset: float32 [1536], P('tensor'), may hold values from -3 to 3
- conv_bc_weight: float32 [4, 256], replicated, may hold values from -3 to 3
- conv_bc_offset: float32 [256], replicated, may hold values from -3 to 3
- step_offset: float32 [24], P('tensor'), may hold values from -5 to -1
- decay_log: float32 [24], P('tensor'), may hold values from 0 to 2.7
- skip_gain: float32 [24], P('tensor'), may hold values from 0.5 to 1.5
- out_gain: float32 [1536], P('tensor'), may hold values from 0.5 to 1.5
- output_matrix: bfloat16 [1536, 768], P('tensor'), may hold values from -0.15625 to 0.15625
Outputs:
- block_out: bfloat16 [16, 1024, 768], P('dp')
- tokens_grad: bfloat16 [16, 1024, 768], P('dp')
- grad_norm_gain: float32 [768], replicated
- grad_proj_gate: float32 [768, 1536], P('dp', 'tensor')
- grad_proj_inner: float32 [768, 1536], P('dp', 'tensor')
- grad_proj_bc: float32 [768, 256], P('dp')
- grad_proj_step: float32 [768, 24], P('dp', 'tensor')
- grad_conv_weight: float32 [4, 1536], P(None, 'tensor')
- grad_conv_offset: float32 [1536], P('tensor')
- grad_conv_bc_weight: float32 [4, 256], replicated
- grad_conv_bc_offset: float32 [256], replicated
- grad_step_offset: float32 [24], P('tensor')
- grad_decay_log: float32 [24], P('tensor')
- grad_skip_gain: float32 [24], P('tensor')
- grad_out_gain: float32 [1536], P('tensor')
- grad_proj_out: float32 [1536, 768], P('tensor', 'dp')
The draws below stay inside these ranges and needn't reach their ends.
Inputs may be any that keep to these rules, and one draw needn't show every extreme that they name: `lengths`: positions at or past a sequence's length are padding. Some sequence has exactly 1024 live tokens in every draw. Slot 2i holds sequence 2i; slot 2i+1 holds sequence 2i+1 or the sequence 2j+1, where j is the index of dp that differs from i in its highest bit; perm is its own inverse.
All inputs are finite; a program needn't handle non-finite values.
Results may differ from the reference program's by a relative error of at most 0.0086.
Values may be sent and summed in bfloat16 or wider, within the bound.
No kernel may reach another device: no remote copies, remote signals or barrier semaphores. Data moves between devices by JAX's collectives and lax.ppermute only.
A program may use at most 128 MiB of HBM per device.

```python
import jax
import jax.numpy as jnp
from jax import lax

D = 768
HEADS = 24
HEADDIM = 64
STATE = 128
CONV = 4
LMAX = 1024
SEQ_DEV = 2
INNER = 1536
NSEQ = 16
N_DP = 8


def draw_pairs(key):
    count = SEQ_DEV * N_DP
    half = N_DP // 2
    key_sizes, key_pick = jax.random.split(key)
    sizes = jax.random.randint(key_sizes, (count,), LMAX // 16, LMAX + 1)
    chosen = jax.random.randint(key_pick, (), 0, half)
    owner = jnp.arange(count) // 2
    sizes = jnp.where(owner == chosen, LMAX, sizes)
    sizes = jnp.where(owner == chosen + half, jnp.minimum(sizes, LMAX - 1), sizes)
    even_sizes = sizes[0::2]
    odd_sizes = sizes[1::2]
    devices = jnp.arange(N_DP)
    mates = jnp.bitwise_xor(devices, half)
    loads = even_sizes + odd_sizes
    traded = even_sizes + odd_sizes[mates]
    gap_now = jnp.abs(loads - loads[mates])
    gap_new = jnp.abs(traded - traded[mates])
    swapped = gap_new < gap_now
    odd_source = jnp.where(swapped, 2 * mates + 1, 2 * devices + 1)
    ordering = jnp.stack([2 * devices, odd_source], axis=1).reshape(count)
    return (sizes.astype(jnp.int32), ordering.astype(jnp.int32))


def draw_lengths(key, part):
    return draw_pairs(key)[0]


def draw_perm(key, part):
    return draw_pairs(key)[1]


def shard_levels(rng, shape, cuts, least, high):
    def one(position, parts):
        steps = jax.random.uniform(jax.random.fold_in(jax.random.fold_in(rng, 6), position), (parts,), jnp.float32, least / len(cuts), high / len(cuts))
        return jnp.repeat(jnp.exp(steps), shape[position] // parts).reshape((-1,) + (1,) * (len(shape) - position - 1))

    loudness = one(*cuts[0])
    for cut in cuts[1:]:
        loudness = loudness * one(*cut)
    return loudness


def bell_draw(own_key, shape, scale, limit, pieces=(), kind=jnp.bfloat16):
    array = scale * jax.random.normal(own_key, shape, jnp.float32)
    if pieces:
        array = array * shard_levels(own_key, shape, pieces, -0.22, 0.18)
    return jnp.clip(array, -limit, limit).astype(kind)


def setup_inputs(seed: int = 0) -> dict:
    seeds = jax.random.split(jax.random.key(seed), 19)
    return {
        "tokens": bell_draw(seeds[0], (NSEQ, LMAX, D), 1.0, 6.0, ((0, 8),)),
        "cotangent": bell_draw(seeds[1], (NSEQ, LMAX, D), 1.0, 6.0, ((0, 8),)),
        "lengths": draw_lengths(jax.random.fold_in(seeds[18], 71), 0),
        "perm": draw_perm(jax.random.fold_in(seeds[18], 71), 0),
        "norm_gain": jnp.clip(1.0 + 0.1 * jax.random.normal(seeds[4], (D,), jnp.float32), 0.5, 1.5),
        "proj_gate": bell_draw(seeds[5], (D, INNER), D ** -0.5, 0.21875, ((1, 4),)),
        "proj_inner": bell_draw(seeds[6], (D, INNER), D ** -0.5, 0.21875, ((1, 4),)),
        "state_input_matrix": bell_draw(seeds[7], (D, 2 * STATE), D ** -0.5, 0.21875),
        "stepsize_matrix": bell_draw(seeds[8], (D, HEADS), D ** -0.5, 0.21875, ((1, 4),)),
        "conv_weight": bell_draw(seeds[9], (CONV, INNER), CONV ** -0.5, 3.0, ((1, 4),), jnp.float32),
        "conv_offset": bell_draw(seeds[10], (INNER,), 0.5, 3.0, ((0, 4),), jnp.float32),
        "conv_bc_weight": bell_draw(seeds[11], (CONV, 2 * STATE), CONV ** -0.5, 3.0, (), jnp.float32),
        "conv_bc_offset": bell_draw(seeds[12], (2 * STATE,), 0.5, 3.0, (), jnp.float32),
        "step_offset": jnp.clip(-5.0 + 4.0 * jax.random.uniform(seeds[13], (HEADS,), jnp.float32) ** shard_levels(seeds[13], (HEADS,), ((0, 4),), -0.2, 0.2), -5.0, -1.0),
        "decay_log": jnp.clip(2.7 * jax.random.uniform(seeds[14], (HEADS,), jnp.float32) ** shard_levels(seeds[14], (HEADS,), ((0, 4),), -0.2, 0.2), 0.0, 2.7),
        "skip_gain": jnp.clip(0.5 + 1.0 * jax.random.uniform(seeds[15], (HEADS,), jnp.float32) ** shard_levels(seeds[15], (HEADS,), ((0, 4),), -0.2, 0.2), 0.5, 1.5),
        "out_gain": jnp.clip(1.0 + 0.1 * jax.random.normal(seeds[16], (INNER,), jnp.float32), 0.5, 1.5),
        "output_matrix": bell_draw(seeds[17], (INNER, D), INNER ** -0.5, 0.15625, ((0, 4),)),
    }


@jax.custom_vjp
def low(v):
    return lax.optimization_barrier(v.astype(jnp.bfloat16)).astype(jnp.float32)

@jax.custom_vjp
def low_back(v):
    return v

def low_keep(v):
    return (low(v), None)

def low_pass(kept, grad):
    return (grad,)

def back_keep(v):
    return (v, None)

def back_low(kept, grad):
    return (low(grad),)
low.defvjp(low_keep, low_pass)
low_back.defvjp(back_keep, back_low)
EPS = 1e-05
HIGH = lax.Precision.HIGHEST

def product(left, right):
    return jnp.dot(left, right, precision=HIGH, preferred_element_type=jnp.float32)

def conv_act(before, weight, offset):
    width = weight.shape[0]
    length = before.shape[0]
    padded = jnp.pad(before, ((width - 1, 0), (0, 0)))
    summed = offset + weight[0] * padded[0:length]
    for tap in range(1, width):
        summed = summed + weight[tap] * padded[tap:tap + length]
    return jax.nn.silu(summed)

def sequence_scan(values, bmat, cmat, steps, rate):
    length = values.shape[0]
    cumul = jnp.cumsum(steps * rate, axis=0).T
    places = jnp.arange(length)
    causal = places[:, None] >= places[None, :]
    spread = cumul[:, :, None] - cumul[:, None, :]
    weights = jnp.exp(jnp.where(causal[None], spread, -1e+30))
    scores = product(cmat, bmat.T)
    mixing = weights * scores[None] * steps.T[:, None, :]
    return jnp.einsum('hts,shp->thp', mixing, values, precision=HIGH)

def block(row, live_mask, norm_gain, proj_gate, proj_inner, state_input_matrix, stepsize_matrix, conv_weight, conv_offset, conv_bc_weight, conv_bc_offset, step_offset, decay_log, skip_gain, out_gain, output_matrix):
    inv_rms = lax.rsqrt(lax.optimization_barrier(jnp.mean(row * row, axis=-1, keepdims=True)) + EPS)
    normalized_rows = low(row * inv_rms * norm_gain)
    gate_pre = low_back(product(normalized_rows, proj_gate))
    inner_pre = low_back(product(normalized_rows, proj_inner))
    state_input_before = low_back(product(normalized_rows, state_input_matrix))
    stepsize_before = low_back(product(normalized_rows, stepsize_matrix))
    active = conv_act(inner_pre, conv_weight, conv_offset)
    bc_act = conv_act(state_input_before, conv_bc_weight, conv_bc_offset)
    steps = jax.nn.softplus(stepsize_before + step_offset)
    length = row.shape[0]
    values = active.reshape(length, HEADS, HEADDIM)
    scanned = sequence_scan(values, bc_act[:, :STATE], bc_act[:, STATE:], steps, -jnp.exp(decay_log))
    scanned = scanned + skip_gain[None, :, None] * values
    gated = scanned.reshape(length, INNER) * jax.nn.silu(gate_pre)
    rgate = lax.rsqrt(lax.optimization_barrier(jnp.mean(gated * gated, axis=-1, keepdims=True)) + EPS)
    gated_rms_output = low(gated * rgate * out_gain)
    return row + live_mask[:, None] * product(gated_rms_output, output_matrix)

def reference(tokens, cotangent, lengths, perm, norm_gain, proj_gate, proj_inner, state_input_matrix, stepsize_matrix, conv_weight, conv_offset, conv_bc_weight, conv_bc_offset, step_offset, decay_log, skip_gain, out_gain, output_matrix):
    params = tuple((p.astype(jnp.float32) for p in (norm_gain, proj_gate, proj_inner, state_input_matrix, stepsize_matrix, conv_weight, conv_offset, conv_bc_weight, conv_bc_offset, step_offset, decay_log, skip_gain, out_gain, output_matrix)))
    dealt = tokens.astype(jnp.float32)[perm]
    cot_float = cotangent.astype(jnp.float32)
    places = jnp.arange(LMAX)
    masks = (places[None, :] < lengths[perm][:, None]).astype(jnp.float32)

    def one_step(totals, item):
        row, row_cot, live_mask = item

        def run(row_in, params_in):
            return block(row_in, live_mask, *params_in)
        result, pull = jax.vjp(run, row, params)
        row_grad, param_grads = pull(row_cot)
        totals = jax.tree.map(jnp.add, totals, param_grads)
        return (totals, (result, row_grad))
    zeros = tuple((jnp.zeros_like(p) for p in params))
    totals, (results, row_grads) = lax.scan(one_step, zeros, (dealt, cot_float, masks))
    tokens_grad = jnp.zeros_like(row_grads).at[perm].set(row_grads)
    return (results.astype(jnp.bfloat16), tokens_grad.astype(jnp.bfloat16), totals[0], totals[1], totals[2], totals[3], totals[4], totals[5], totals[6], totals[7], totals[8], totals[9], totals[10], totals[11], totals[12], totals[13])
```

```python
import functools

import numpy as np
import jax
import jax.numpy as jnp
from jax import lax
from jax.experimental import pallas as pl
from jax.experimental.pallas import tpu as pltpu
from jax.sharding import PartitionSpec as P

EPS = 1e-05
SUB = 128
ROWS = 256
HP = 8
F32 = jnp.float32
BF = jnp.bfloat16
HIGH = lax.Precision.HIGHEST
NT = (((1,), (1,)), ((), ()))
TN = (((0,), (0,)), ((), ()))


def dot(a, b, dims=(((1,), (0,)), ((), ())), precision=None):
    return lax.dot_general(a, b, dims, precision=precision, preferred_element_type=F32)


def sigmoid(v):
    return 1.0 / (1.0 + jnp.exp(-v))


def split(v):
    high = v.astype(BF).astype(F32)
    return high, (v - high).astype(BF).astype(F32)


def spread_matrix(heads, hsize, kinds):
    inner = heads * hsize
    out = np.zeros((2, kinds, HP, kinds, heads, hsize), np.float32)
    for kind in range(kinds):
        for head in range(heads):
            out[:, kind, head, kind, head] = 1
    return out.reshape(2 * kinds * HP, kinds * inner)


def gather_matrix(heads, hsize):
    inner = heads * hsize
    out = np.zeros((4, heads, hsize, 128), np.float32)
    for part, base in enumerate((0, 0, HP, 2 * HP)):
        for head in range(heads):
            out[part, head, :, base + head] = 1
    return out.reshape(4 * inner, 128)


def spread(rows, matrix):
    parts = [split(r) for r in rows]
    stack = jnp.concatenate([p[0] for p in parts] + [p[1] for p in parts], axis=0)
    wide = dot(stack.T.astype(BF), matrix)
    inner = wide.shape[1] // len(rows)
    return [wide[:, k * inner : (k + 1) * inner] for k in range(len(rows))]


def pair_blocks(values, low_lanes):
    zero = jnp.zeros_like(values)
    return jnp.concatenate([jnp.where(low_lanes, values, zero), jnp.where(low_lanes, zero, values)], axis=0)


def fwd_kernel(
    tok_ref, gain_ref, w_ref, wst_ref, cw_ref, cb_ref, hp_ref, skip_ref, og_ref, wout_ref, spread_ref,
    p_ref, sq_ref, sg_ref, gy_ref, gated_ref, yi_ref, yo_ref, x_ref, xs_ref, bc_ref, dsil_ref, pre_ref,
    rows_ref, sin_ref, normed_ref,
    buf, state,
):
    rows = tok_ref.shape[0]
    inner = og_ref.shape[1]
    nstate = state.shape[0]
    wide = buf.shape[1]
    heads = inner // 64

    @pl.when(pl.program_id(0) == 0)
    def _():
        state[...] = jnp.zeros_like(state)
        buf[0:8, :] = jnp.zeros((8, wide), F32)

    tok = tok_ref[...].astype(F32)
    rstd = lax.rsqrt(jnp.mean(tok * tok, axis=-1, keepdims=True) + EPS)
    normed = (tok * rstd * gain_ref[...]).astype(BF)
    normed_ref[...] = normed
    pre = dot(normed, w_ref[...])
    gate_pre = pre[:, :inner]
    buf[8 : 8 + rows, :] = pre[:, inner:]
    pre_ref[...] = pre[:, inner:].astype(pre_ref.dtype)
    step_pre = dot(wst_ref[...], normed, NT) + hp_ref[:, 0:1]
    steps = jnp.maximum(step_pre, 0.0) + jnp.log1p(jnp.exp(-jnp.abs(step_pre)))
    rows_ref[0:HP, :] = steps
    rows_ref[2 * HP : 3 * HP, :] = sigmoid(step_pre)
    rates = steps * hp_ref[:, 1:2]

    conv = cb_ref[...] + cw_ref[0:1, :] * buf[5 : 5 + rows, :]
    for tap in range(1, 4):
        conv = conv + cw_ref[tap : tap + 1, :] * buf[5 + tap : 5 + tap + rows, :]
    buf[0:8, :] = buf[rows : rows + 8, :]
    sig = sigmoid(conv)
    act = conv * sig
    dsil_ref[...] = (sig * (1.0 + conv * (1.0 - sig))).astype(dsil_ref.dtype)
    x = act[:, :inner]
    x_ref[...] = x.astype(x_ref.dtype)
    bc = act[:, inner:].astype(BF)
    bc_ref[...] = bc

    at_row = lax.broadcasted_iota(jnp.int32, (SUB, SUB), 0)
    at_col = lax.broadcasted_iota(jnp.int32, (SUB, SUB), 1)
    causal = at_row >= at_col
    upper = (at_row <= at_col).astype(F32)
    low_lanes = lax.broadcasted_iota(jnp.int32, (SUB, 128), 1) < 64
    gsig = sigmoid(gate_pre)
    sgate = gate_pre * gsig
    dgate = gsig * (1.0 + gate_pre * (1.0 - gsig))
    for sub in range(rows // SUB):
        here = slice(sub * SUB, (sub + 1) * SUB)
        cum = dot(rates[:, here], upper, precision=HIGH)
        rows_ref[HP : 2 * HP, here] = cum
        cum_col = cum.T
        step_x, ecum_x, eend_x = spread(
            [steps[:, here], jnp.exp(cum), jnp.exp(cum[:, SUB - 1 : SUB] - cum)], spread_ref[...]
        )
        bmat = bc[here, :nstate]
        cmat = bc[here, nstate:]
        xs = x[here] * step_x
        xsb = xs.astype(BF)
        xs_ref[here, :] = xsb
        scores = dot(cmat, bmat, NT)
        inside = []
        for pair in range(heads // 2):
            mix = []
            for head in (2 * pair, 2 * pair + 1):
                gap = cum_col[:, head : head + 1] - cum[head : head + 1, :]
                mix.append((jnp.exp(jnp.where(causal, gap, -1e30)) * scores).astype(BF))
            blocks = pair_blocks(xsb[:, pair * 128 : (pair + 1) * 128], low_lanes)
            inside.append(dot(jnp.concatenate(mix, axis=1), blocks))
        inside = jnp.concatenate(inside, axis=1)
        yi_ref[here, :] = inside
        enter = state[...]
        enter_b = enter.astype(BF)
        sin_ref[here, :] = enter_b
        outside = dot(cmat, enter_b) * ecum_x
        yo_ref[here, :] = outside.astype(yo_ref.dtype)
        xw = (xs * eend_x).astype(BF)
        state[...] = enter * ecum_x[SUB - 1 : SUB, :] + dot(bmat, xw, TN)
        y = inside + outside + skip_ref[...] * x[here]
        gated = y * sgate[here]
        gy_ref[here, :] = (y * dgate[here]).astype(gy_ref.dtype)
        gated_ref[here, :] = gated.astype(gated_ref.dtype)
        sq_ref[:, here] = dot(jnp.ones((HP, inner), BF), (gated * gated).astype(BF), NT)
        p_ref[here, :] = dot((gated * og_ref[...]).astype(BF), wout_ref[...]).astype(BF)
    sg_ref[...] = sgate.astype(sg_ref.dtype)


def mid_kernel(len_ref, cot_ref, gated_ref, sq_ref, og_ref, wout_ref, nog_ref, stat_ref):
    rows = cot_ref.shape[0]
    first = pl.program_id(0) * rows
    live = first + lax.broadcasted_iota(jnp.int32, (rows, 1), 0) < len_ref[0]
    branch_grad = jnp.where(live, cot_ref[...], jnp.zeros((), BF))
    nog = dot(branch_grad, wout_ref[...], NT)
    nog_ref[...] = nog.astype(nog_ref.dtype)
    inner = og_ref.shape[1]
    cross = nog * og_ref[...] * gated_ref[...].astype(F32)
    sums = dot(jnp.ones((HP, inner), BF), cross.astype(BF), NT)
    top = lax.broadcasted_iota(jnp.int32, (HP, rows), 0) == 0
    stat_ref[...] = jnp.where(top, sq_ref[...], sums)


def bwd_kernel(
    inner_all,
    len_ref, tok_ref, gain_ref, w_ref, wst_ref, cw_ref, hp_ref, skip_ref, og_ref, spread_ref, gather_ref,
    stat_ref, nog_ref, sg_ref, gy_ref, gated_ref, yi_ref, yo_ref, x_ref, xs_ref, bc_ref, dsil_ref, pre_ref,
    rows_ref, sin_ref,
    joint_ref, stepg_ref, n_ref, gnorm_ref, gconv_ref, ggain_ref, gog_ref, gskip_ref, ghead_ref,
    buf, dstate,
):
    rows = tok_ref.shape[0]
    inner = og_ref.shape[1]
    nstate = dstate.shape[0]
    wide = buf.shape[1]
    heads = inner // 64
    turn = pl.program_id(0)
    first = (pl.num_programs(0) - 1 - turn) * rows

    @pl.when(turn == 0)
    def _():
        dstate[...] = jnp.zeros_like(dstate)
        buf[rows : rows + 8, :] = jnp.zeros((8, wide), F32)
        for ref in (gconv_ref, ggain_ref, gog_ref, gskip_ref, ghead_ref):
            ref[...] = jnp.zeros_like(ref)

    at_row = lax.broadcasted_iota(jnp.int32, (SUB, SUB), 0)
    at_col = lax.broadcasted_iota(jnp.int32, (SUB, SUB), 1)
    causal_t = at_row <= at_col
    lower = (at_row >= at_col).astype(F32)
    upper_strict = (at_row < at_col).astype(F32)
    low_lanes = lax.broadcasted_iota(jnp.int32, (SUB, 128), 1) < 64
    last_row = lax.broadcasted_iota(jnp.int32, (SUB, 1), 0) == SUB - 1
    og = og_ref[...]
    skip = skip_ref[...]

    for sub in reversed(range(rows // SUB)):
        here = slice(sub * SUB, (sub + 1) * SUB)
        stat = stat_ref[:, here]
        rg = lax.rsqrt(stat[0:1, :] * (1.0 / inner_all) + EPS)
        coef = rg * rg * rg * stat[1:2, :] * (1.0 / inner_all)
        cols = jnp.concatenate([rg, coef, jnp.zeros((6, SUB), F32)], axis=0).T
        rgate = cols[:, 0:1]
        gated = gated_ref[here, :].astype(F32)
        nog = nog_ref[here, :].astype(F32)
        live = first + sub * SUB + lax.broadcasted_iota(jnp.int32, (SUB, 1), 0) < len_ref[0]
        ghat = gated * rgate
        gnorm_ref[here, :] = jnp.where(live, ghat * og, 0.0).astype(BF)
        gog_ref[0:1, :] += jnp.sum(nog * ghat, axis=0, keepdims=True)
        gg = rgate * (nog * og) - gated * cols[:, 1:2]
        joint_ref[here, :inner] = (gg * gy_ref[here, :].astype(F32)).astype(BF)
        dyb = (gg * sg_ref[here, :].astype(F32)).astype(BF)
        dy = dyb.astype(F32)

        steps = rows_ref[0:HP, here]
        cum = rows_ref[HP : 2 * HP, here]
        cum_col = cum.T
        step_x, ecum_x, eend_x = spread(
            [steps, jnp.exp(cum), jnp.exp(cum[:, SUB - 1 : SUB] - cum)], spread_ref[...]
        )
        bmat = bc_ref[here, :nstate]
        cmat = bc_ref[here, nstate:]
        xsb = xs_ref[here, :]
        xs = xsb.astype(F32)
        xf = x_ref[here, :].astype(F32)
        scores_t = dot(bmat, cmat, NT)
        dscores_t = jnp.zeros((SUB, SUB), F32)
        dxs_in = []
        for pair in range(heads // 2):
            lanes = slice(pair * 128, (pair + 1) * 128)
            mix = []
            dy_blocks = pair_blocks(dyb[:, lanes], low_lanes)
            for head in (2 * pair, 2 * pair + 1):
                gap = cum[head : head + 1, :] - cum_col[:, head : head + 1]
                weight = jnp.exp(jnp.where(causal_t, gap, -1e30))
                mix.append((weight * scores_t).astype(BF))
                part = head - 2 * pair
                dmix = dot(xsb[:, lanes], dy_blocks[part * SUB : (part + 1) * SUB, :], NT)
                dscores_t = dscores_t + dmix * weight
            dxs_in.append(dot(jnp.concatenate(mix, axis=1), dy_blocks))
        dxs_in = jnp.concatenate(dxs_in, axis=1)
        dleave = dstate[...]
        dleave_b = dleave.astype(BF)
        enter_b = sin_ref[here, :]
        xwb = (xs * eend_x).astype(BF)
        dye = (dy * ecum_x).astype(BF)
        dsc = dscores_t.astype(BF)
        dxw = dot(bmat, dleave_b)
        dbm = dot(dsc, cmat) + dot(xwb, dleave_b, NT)
        dcm = dot(dsc, bmat, TN) + dot(dye, enter_b, NT)
        dxs = dxs_in + eend_x * dxw
        dx = step_x * dxs + skip * dy
        gskip_ref[0:1, :] += jnp.sum(dy * xf, axis=0, keepdims=True)
        z1 = dy * (yi_ref[here, :] + yo_ref[here, :].astype(F32)) - xs * dxs_in
        ends = ecum_x[SUB - 1 : SUB, :]
        carry = jnp.sum(enter_b.astype(F32) * dleave, axis=0, keepdims=True) * ends
        z1 = z1 + jnp.where(last_row, carry, 0.0)
        z1h, z1l = split(z1)
        packed = jnp.concatenate(
            [z1h.astype(BF), z1l.astype(BF), (xwb.astype(F32) * dxw).astype(BF), (xf * dxs).astype(BF)], axis=1
        )
        sums = dot(packed, gather_ref[...]).T
        da = dot(sums[0:HP], lower, precision=HIGH) + dot(sums[HP : 2 * HP], upper_strict, precision=HIGH)
        dstate[...] = dleave * ends + dot(cmat, dye, TN)
        rate = hp_ref[:, 1:2]
        dstep_pre = (rate * da + sums[2 * HP : 3 * HP]) * rows_ref[2 * HP : 3 * HP, here]
        stepg_ref[:, here] = dstep_pre.astype(BF).astype(F32)
        ghead_ref[0:HP, :] += dstep_pre
        ghead_ref[HP : 2 * HP, :] += da * steps * rate
        buf[here, :inner] = dx * dsil_ref[here, :inner].astype(F32)
        buf[here, inner:] = jnp.concatenate([dbm, dcm], axis=1) * dsil_ref[here, inner:].astype(F32)

    pre = pre_ref[...].astype(F32)
    back = jnp.zeros((rows, wide), F32)
    for tap in range(4):
        moved = buf[3 - tap : 3 - tap + rows, :]
        back = back + cw_ref[tap : tap + 1, :] * moved
        gconv_ref[tap : tap + 1, :] += jnp.sum(moved * pre, axis=0, keepdims=True)
    gconv_ref[4:5, :] += jnp.sum(buf[0:rows, :], axis=0, keepdims=True)
    buf[rows : rows + 8, :] = buf[0:8, :]
    joint_ref[:, inner:] = back.astype(BF)
    grad = dot(joint_ref[...], w_ref[...], NT) + dot(stepg_ref[...].astype(BF), wst_ref[...], TN)
    n_ref[...] = grad.astype(BF)
    tok = tok_ref[...].astype(F32)
    hat = tok * lax.rsqrt(jnp.mean(tok * tok, axis=-1, keepdims=True) + EPS)
    ggain_ref[0:1, :] += jnp.sum(grad * hat, axis=0, keepdims=True)


def whole(shape):
    return pl.BlockSpec(shape, lambda i: (0,) * len(shape))


def down(shape, blocks=0):
    if blocks:
        return pl.BlockSpec(shape, lambda i: (blocks - 1 - i, 0))
    return pl.BlockSpec(shape, lambda i: (i, 0))


def across(shape, blocks=0):
    if blocks:
        return pl.BlockSpec(shape, lambda i: (0, blocks - 1 - i))
    return pl.BlockSpec(shape, lambda i: (0, i))


PARAMS = pltpu.CompilerParams(vmem_limit_bytes=48 * 1024 * 1024)


def forward(tok, gain, w, wst, cw, cb, hp, skip, og, wout, spread_m, nstate):
    length, width = tok.shape
    inner = og.shape[1]
    wide = cw.shape[1]
    sds = jax.ShapeDtypeStruct
    r = ROWS
    outs = [
        (sds((length, width), BF), down((r, width))),
        (sds((HP, length), F32), across((HP, r))),
        (sds((length, inner), F32), down((r, inner))),
        (sds((length, inner), F32), down((r, inner))),
        (sds((length, inner), F32), down((r, inner))),
        (sds((length, inner), F32), down((r, inner))),
        (sds((length, inner), F32), down((r, inner))),
        (sds((length, inner), F32), down((r, inner))),
        (sds((length, inner), BF), down((r, inner))),
        (sds((length, 2 * nstate), BF), down((r, 2 * nstate))),
        (sds((length, wide), F32), down((r, wide))),
        (sds((length, wide), F32), down((r, wide))),
        (sds((3 * HP, length), F32), across((3 * HP, r))),
        (sds((length, inner), BF), down((r, inner))),
        (sds((length, width), BF), down((r, width))),
    ]
    ins = [tok, gain, w, wst, cw, cb, hp, skip, og, wout, spread_m]
    return pl.pallas_call(
        fwd_kernel,
        grid=(length // r,),
        in_specs=[down((r, width))] + [whole(v.shape) for v in ins[1:]],
        out_specs=[o[1] for o in outs],
        out_shape=[o[0] for o in outs],
        scratch_shapes=[pltpu.VMEM((r + 8, wide), F32), pltpu.VMEM((nstate, inner), F32)],
        compiler_params=PARAMS,
        name="forward",
    )(*ins)


def middle(live, cot, gated, sq, og, wout):
    length, width = cot.shape
    inner = og.shape[1]
    r = ROWS
    return pl.pallas_call(
        mid_kernel,
        grid=(length // r,),
        in_specs=[
            pl.BlockSpec(memory_space=pltpu.SMEM), down((r, width)), down((r, inner)), across((HP, r)),
            whole(og.shape), whole(wout.shape),
        ],
        out_specs=[down((r, inner)), across((HP, r))],
        out_shape=[
            jax.ShapeDtypeStruct((length, inner), F32), jax.ShapeDtypeStruct((HP, length), F32),
        ],
        compiler_params=PARAMS,
        name="middle",
    )(live, cot, gated, sq, og, wout)


def backward(live, tok, gain, w, wst, cw, hp, skip, og, spread_m, gather_m, stat, nog, kept, inner_all):
    length, width = tok.shape
    inner = og.shape[1]
    wide = cw.shape[1]
    nstate = (wide - inner) // 2
    sg, gy, gated, yi, yo, x, xs, bc, dsil, pre, rowsv, sin = kept
    r = ROWS
    n = length // r
    sds = jax.ShapeDtypeStruct
    consts = [gain, w, wst, cw, hp, skip, og, spread_m, gather_m]
    tall = [nog, sg, gy, gated, yi, yo, x, xs, bc, dsil, pre]
    outs = [
        (sds((length, inner + wide), BF), down((r, inner + wide), n)),
        (sds((HP, length), F32), across((HP, r), n)),
        (sds((length, width), BF), down((r, width), n)),
        (sds((length, inner), BF), down((r, inner), n)),
        (sds((8, wide), F32), whole((8, wide))),
        (sds((8, width), F32), whole((8, width))),
        (sds((8, inner), F32), whole((8, inner))),
        (sds((8, inner), F32), whole((8, inner))),
        (sds((2 * HP, SUB), F32), whole((2 * HP, SUB))),
    ]
    return pl.pallas_call(
        functools.partial(bwd_kernel, inner_all),
        grid=(n,),
        in_specs=[pl.BlockSpec(memory_space=pltpu.SMEM), down((r, width), n)]
        + [whole(v.shape) for v in consts]
        + [across((HP, r), n)]
        + [down((r, v.shape[1]), n) for v in tall]
        + [across((3 * HP, r), n), down((r, inner), n)],
        out_specs=[o[1] for o in outs],
        out_shape=[o[0] for o in outs],
        scratch_shapes=[pltpu.VMEM((r + 8, wide), F32), pltpu.VMEM((nstate, inner), F32)],
        compiler_params=PARAMS,
        name="backward",
    )(live, tok, *consts, stat, *tall, rowsv, sin)


def swap(value, axis, bit):
    mask = 1 << bit
    return lax.ppermute(value, axis, [(i, i ^ mask) for i in range(lax.axis_size(axis))])


def bits(axis):
    return lax.axis_size(axis).bit_length() - 1


def sum_over(value, axis):
    for bit in range(bits(axis)):
        value = value + swap(value, axis, bit)
    return value


def half_of(value, which):
    size = value.shape[0] // 2
    return lax.dynamic_slice_in_dim(value, which * size, size, 0)


def join(mine, other, which):
    return jnp.where(which == 0, jnp.concatenate([mine, other], 0), jnp.concatenate([other, mine], 0))


def sum_half(partial, core):
    got = swap(half_of(partial, 1 - core), "tensor", 0)
    total = (half_of(partial, core).astype(F32) + got.astype(F32)).astype(BF)
    for bit in range(1, bits("tensor")):
        more = swap(total, "tensor", bit)
        if bit == bits("tensor") - 1:
            return total.astype(F32) + more.astype(F32)
        total = (total.astype(F32) + more.astype(F32)).astype(BF)


def scatter_rows(value):
    place = lax.axis_index("dp")
    nbits = bits("dp")
    rows = value.shape[0] >> nbits
    total = value.reshape((1 << nbits, rows) + value.shape[1:])
    for bit in range(nbits):
        mine = (place >> bit) & 1
        pairs = total.reshape((total.shape[0] // 2, 2) + total.shape[1:])
        keep = lax.dynamic_index_in_dim(pairs, mine, 1, keepdims=False)
        give = lax.dynamic_index_in_dim(pairs, 1 - mine, 1, keepdims=False)
        got = swap(give, "dp", bit)
        total = keep.astype(F32) + got.astype(F32)
        if bit < nbits - 1:
            total = total.astype(BF)
    return total[0]


def body(
    tokens, cotangent, lengths, perm, norm_gain, proj_gate, proj_inner, state_input_matrix, stepsize_matrix,
    conv_weight, conv_offset, conv_bc_weight, conv_bc_offset, step_offset, decay_log, skip_gain, out_gain,
    output_matrix,
):
    slots, length, width = tokens.shape
    inner = proj_gate.shape[1]
    heads = step_offset.shape[0]
    hsize = inner // heads
    nstate = state_input_matrix.shape[1] // 2
    inner_all = inner * lax.axis_size("tensor")
    place = lax.axis_index("dp")
    core = lax.axis_index("tensor") & 1
    top = bits("dp") - 1
    first = place * slots
    moved = lax.dynamic_index_in_dim(perm, first + 1, 0, keepdims=False) != first + 1

    w = jnp.concatenate([proj_gate, proj_inner, state_input_matrix], axis=1)
    wst = jnp.pad(stepsize_matrix.T, ((0, HP - heads), (0, 0)))
    cw = jnp.pad(jnp.concatenate([conv_weight, conv_bc_weight], axis=1), ((0, 4), (0, 0)))
    cb = jnp.concatenate([conv_offset, conv_bc_offset])[None]
    hp = jnp.pad(jnp.stack([step_offset, -jnp.exp(decay_log)], axis=1), ((0, HP - heads), (0, 126)))
    skip = jnp.repeat(skip_gain, hsize)[None]
    og = out_gain[None]
    gain = norm_gain[None]
    spread_m = jnp.asarray(spread_matrix(heads, hsize, 3), BF)
    gather_m = jnp.asarray(gather_matrix(heads, hsize), BF)

    far = swap(half_of(cotangent[1], core), "dp", top)
    near = swap(far, "tensor", 0)
    cots = [cotangent[0], jnp.where(moved, join(far, near, core), cotangent[1])]

    kept, partial, stats, nogs, lives = [], [], [], [], []
    for slot in range(slots):
        out = forward(tokens[slot], gain, w, wst, cw, cb, hp, skip, og, output_matrix, spread_m, nstate)
        partial.append(out[0])
        kept.append(out)
        live = lax.dynamic_slice_in_dim(lengths, first + slot, 1, 0)
        lives.append(live)
        nog, stat = middle(live, cots[slot], out[4], out[1], og, output_matrix)
        nogs.append(nog)
        stats.append(sum_over(stat, "tensor"))

    block_halves = []
    for slot in range(slots):
        branch = sum_half(partial[slot], core)
        rg = lax.rsqrt(half_of(stats[slot][0], core) / inner_all + EPS)
        mask = core * (length // 2) + jnp.arange(length // 2) < lives[slot][0]
        block = half_of(tokens[slot], core).astype(F32) + jnp.where(mask, rg, 0.0)[:, None] * branch
        block_halves.append(block.astype(BF))
    away = swap(block_halves[1], "dp", top)
    block_halves[1] = jnp.where(moved, away, block_halves[1])
    block_out = jnp.stack([join(b, swap(b, "tensor", 0), core) for b in block_halves])

    grads, results = [], []
    for slot in range(slots):
        res = backward(
            lives[slot], tokens[slot], gain, w, wst, cw, hp, skip, og, spread_m, gather_m, stats[slot], nogs[slot],
            kept[slot][2:14], inner_all,
        )
        results.append(res)
        normed_grad = sum_half(res[2], core)
        tok = half_of(tokens[slot], core).astype(F32)
        rstd = lax.rsqrt(jnp.mean(tok * tok, axis=-1, keepdims=True) + EPS)
        hat = tok * rstd
        lifted = normed_grad * norm_gain
        dealt_grad = rstd * (lifted - hat * jnp.mean(lifted * hat, axis=-1, keepdims=True))
        own = (half_of(cots[slot], core).astype(F32) + dealt_grad).astype(BF)
        grads.append(join(own, swap(own, "tensor", 0), core))
    tokens_grad = jnp.stack(grads)

    normed = jnp.concatenate([k[14] for k in kept], axis=0)
    joint = jnp.concatenate([r[0] for r in results], axis=0)
    gnorm = jnp.concatenate([r[3] for r in results], axis=0)
    cot_all = jnp.concatenate(cots, axis=0)
    stepg = jnp.concatenate([r[1] for r in results], axis=1).astype(BF)
    dw = dot(normed, joint, TN)
    dwo = dot(cot_all, gnorm, TN)
    dws = dot(stepg, normed).T
    packed = jnp.concatenate([dw, dwo, dws], axis=1).astype(BF)
    mine = scatter_rows(packed)
    wide = 2 * nstate
    small = [sum(r[k] for r in results) for k in range(4, 9)]
    gconv, ggain, gog, gskip, ghead = small
    ghead = jnp.sum(ghead, axis=1)
    gskip = jnp.sum(gskip[0].reshape(heads, hsize), axis=1)
    both = jnp.concatenate([ggain[0], gconv[:5, inner:].reshape(-1)])
    alone = jnp.concatenate(
        [gconv[:5, :inner].reshape(-1), gog[0], ghead[:heads], ghead[HP : HP + heads], gskip]
    )
    cut = both.shape[0]
    everything = sum_over(jnp.concatenate([both, alone]), "dp")
    bc_shard = mine[:, 2 * inner : 2 * inner + wide]
    summed = sum_over(jnp.concatenate([bc_shard.reshape(-1), everything[:cut]]), "tensor")
    both = summed[bc_shard.size :]
    alone = everything[cut:]
    conv_both = both[width:].reshape(5, wide)
    conv_own = alone[: 5 * inner].reshape(5, inner)
    tail = alone[5 * inner :]
    return (
        block_out,
        tokens_grad,
        both[:width],
        mine[:, :inner],
        mine[:, inner : 2 * inner],
        summed[: bc_shard.size].reshape(bc_shard.shape),
        mine[:, 3 * inner + wide : 3 * inner + wide + heads],
        conv_own[:4],
        conv_own[4],
        conv_both[:4],
        conv_both[4],
        tail[inner : inner + heads],
        tail[inner + heads : inner + 2 * heads],
        tail[inner + 2 * heads :],
        tail[:inner],
        mine[:, 2 * inner + wide : 3 * inner + wide].T,
    )


def solution(mesh):
    return jax.shard_map(
        body,
        mesh=mesh,
        in_specs=(
            P("dp", None, None), P("dp", None, None), P(), P(), P(), P(None, "tensor"), P(None, "tensor"), P(),
            P(None, "tensor"), P(None, "tensor"), P("tensor"), P(), P(), P("tensor"), P("tensor"), P("tensor"),
            P("tensor"), P("tensor", None),
        ),
        out_specs=(
            P("dp", None, None), P("dp", None, None), P(), P("dp", "tensor"), P("dp", "tensor"), P("dp", None),
            P("dp", "tensor"), P(None, "tensor"), P("tensor"), P(), P(), P("tensor"), P("tensor"), P("tensor"),
            P("tensor"), P("tensor", "dp"),
        ),
        check_vma=False,
    )
```
